512 devices in a mesh: dp: 8 (over y_hi, core), expert: 64 (over z, y_lo, x).
Axes of the slice: x: 4, y: 8 (y_hi: 4, y_lo: 2; y = y_hi * 2 + y_lo), z: 8, core: 2. Of those that a mesh axis runs over, the one named last changes fastest.
Arguments:
- tokens: bfloat16 [4096, 2048], P('expert', 'dp'), may hold values from -6 to 6
- expert_ids: int32 [4096, 8], P('expert'), may hold values from 0 to 63, as said below
- router_probs: float32 [4096, 8], P('expert'), may hold values from 0.05 to 1
- w_gate: bfloat16 [64, 2048, 3072], P('expert', None, 'dp'), may hold values from -0.125 to 0.125
- w_up: bfloat16 [64, 2048, 3072], P('expert', None, 'dp'), may hold values from -0.125 to 0.125
- w_down: bfloat16 [64, 3072, 2048], P('expert', 'dp'), may hold values from -0.109375 to 0.109375
Outputs:
- mixed: bfloat16 [4096, 2048], P('expert', 'dp')
The draws below stay inside these ranges and needn't reach their ends.
Inputs may be any that keep to these rules, and one draw needn't show every extreme that they name: `expert_ids`: A row's 8 ids differ. In each aligned block of 64 rows (the rows of one device) no expert is named more than 12 times; 8 experts, the same in all blocks and chosen by the seed, are named exactly 12 times in every block; every expert is named somewhere.
All inputs are finite; a program needn't handle non-finite values.
Results may differ from the reference program's by a relative error of at most 0.02.
Values may be sent and summed in bfloat16 or wider, within the bound.
No kernel may reach another device: no remote copies, remote signals or barrier semaphores. Data moves between devices by JAX's collectives and lax.ppermute only.
A program may use at most 64 MiB of HBM per device.

```python
import math
import jax
import jax.numpy as jnp
from jax import lax

D = 2048
F = 3072
TOP = 8
TOK_DEV = 64
EXPERTS = 64
C = 12
HOT = 8
TOKENS = 4096
N_DP = 8


def draw_expert_ids(key, part):
    key = jax.random.fold_in(key, 11)
    hot_key, block_key = jax.random.split(key)
    seat_total = EXPERTS * C
    ranking = jax.random.permutation(hot_key, EXPERTS)
    hot_flag = jnp.zeros((EXPERTS,), jnp.int32).at[ranking[:HOT]].set(1)
    seat_expert = (jnp.arange(seat_total, dtype=jnp.int32) // C).astype(jnp.int32)
    seat_hot = hot_flag[seat_expert]
    drop_count = seat_total - TOK_DEV * TOP

    def one_block(this_key):
        key_seats, key_rows, key_cols = jax.random.split(this_key, 3)
        score = jax.random.permutation(key_seats, seat_total).astype(jnp.int32)
        score = jnp.where(seat_hot == 1, score + seat_total, score)
        ranked = jnp.argsort(jnp.argsort(score)).astype(jnp.int32)
        keep_seat = ranked >= drop_count
        placed = jnp.cumsum(keep_seat.astype(jnp.int32)) - 1
        target = jnp.where(keep_seat, placed, TOK_DEV * TOP)
        sequence = jnp.zeros((TOK_DEV * TOP,), jnp.int32).at[target].set(seat_expert, mode='drop')
        id_grid = sequence.reshape(TOP, TOK_DEV).T
        id_grid = id_grid[jax.random.permutation(key_rows, TOK_DEV)]
        col_scores = jax.random.randint(key_cols, (TOK_DEV, TOP), 0, 1 << 20) * TOP + jnp.arange(TOP, dtype=jnp.int32)[None, :]
        col_order = jnp.argsort(col_scores, axis=1)
        return jnp.take_along_axis(id_grid, col_order, axis=1)
    block_keys = jax.random.split(block_key, TOKENS // TOK_DEV)
    return jax.vmap(one_block)(block_keys).reshape(TOKENS, TOP).astype(jnp.int32)


def shard_levels(rng, dims, shards, low, largest):
    def one(axis_at, blocks):
        steps = jax.random.uniform(jax.random.fold_in(jax.random.fold_in(rng, 6), axis_at), (blocks,), jnp.float32, low / len(shards), largest / len(shards))
        return jnp.repeat(jnp.exp(steps), dims[axis_at] // blocks).reshape((-1,) + (1,) * (len(dims) - axis_at - 1))

    factor_of = one(*shards[0])
    for cut in shards[1:]:
        factor_of = factor_of * one(*cut)
    return factor_of


def centred(rng, extent, spread, limit, cuts=(), kind=jnp.bfloat16):
    drawn = spread * jax.random.normal(rng, extent, jnp.float32)
    if cuts:
        drawn = drawn * shard_levels(rng, extent, cuts, -0.22, 0.18)
    return jnp.clip(drawn, -limit, limit).astype(kind)


def setup_inputs(seed: int = 0) -> dict:
    streams_of = jax.random.split(jax.random.key(seed), 7)
    tokens = centred(streams_of[0], (TOKENS, D), 1.0, 6.0, ((0, 64), (1, 8)))
    expert_ids = draw_expert_ids(jax.random.fold_in(streams_of[6], 71), 0)
    router_probs = jnp.clip(jnp.exp(math.log(1.0) - 2.9957323 * jax.random.uniform(streams_of[2], (TOKENS, TOP), jnp.float32) ** shard_levels(streams_of[2], (TOKENS, TOP), ((0, 64),), -0.2, 0.2)), 0.05, 1.0)
    w_gate = centred(streams_of[3], (EXPERTS, D, F), D ** -0.5, 0.125, ((0, 64), (2, 8)))
    w_up = centred(streams_of[4], (EXPERTS, D, F), D ** -0.5, 0.125, ((0, 64), (2, 8)))
    w_down = centred(streams_of[5], (EXPERTS, F, D), F ** -0.5, 0.109375, ((0, 64), (1, 8)))
    return {"tokens": tokens, "expert_ids": expert_ids, "router_probs": router_probs, "w_gate": w_gate, "w_up": w_up, "w_down": w_down}


def slot_numbers(expert_ids):
    blocks = expert_ids.reshape(-1, TOK_DEV * TOP)
    labels = jnp.arange(EXPERTS, dtype=jnp.int32)
    onehot = (blocks[:, :, None] == labels[None, None, :]).astype(jnp.int32)
    before = jnp.cumsum(onehot, axis=1) - onehot
    return jnp.sum(before * onehot, axis=2).reshape(expert_ids.shape).astype(jnp.int32)


def reference(tokens, expert_ids, router_probs, w_gate, w_up, w_down):
    slot_no = slot_numbers(expert_ids)
    shares = (router_probs / jnp.sum(router_probs, axis=1, keepdims=True)).astype(jnp.bfloat16)
    seat_count = (TOKENS // TOK_DEV) * C
    blocks = (jnp.arange(TOKENS, dtype=jnp.int32) // TOK_DEV).astype(jnp.int32)
    position = (blocks[:, None] * C + slot_no).astype(jnp.int32)
    token_index = jnp.broadcast_to(jnp.arange(TOKENS, dtype=jnp.int32)[:, None], expert_ids.shape)
    holder = jnp.full((EXPERTS, seat_count), TOKENS, jnp.int32).at[expert_ids, position].set(token_index)
    weight_at = jnp.zeros((EXPERTS, seat_count), jnp.float32).at[expert_ids, position].set(shares.astype(jnp.float32))
    padded = jnp.concatenate([tokens, jnp.zeros((1, D), tokens.dtype)], axis=0)
    slice_width = F // N_DP

    def one_expert(summed, inputs):
        gate_w, up_w, down_w, rows_at, scale_at = inputs
        gathered = padded[rows_at]
        gate_part = jnp.dot(gathered, gate_w, preferred_element_type=jnp.float32)
        up_part = jnp.dot(gathered, up_w, preferred_element_type=jnp.float32)
        hidden = (jax.nn.silu(gate_part) * up_part).astype(jnp.bfloat16)
        pieces = jnp.einsum("rsf,sfd->srd", hidden.reshape(seat_count, N_DP, slice_width).astype(jnp.float32), down_w.reshape(N_DP, slice_width, D).astype(jnp.float32))
        rounded = lax.optimization_barrier(pieces.astype(jnp.bfloat16))
        expert_out = lax.optimization_barrier(jnp.sum(rounded.astype(jnp.float32), axis=0).astype(jnp.bfloat16))
        summed = summed.at[rows_at].add(scale_at[:, None] * expert_out.astype(jnp.float32))
        return summed, None

    start_sum = jnp.zeros((TOKENS + 1, D), jnp.float32)
    summed, unused = lax.scan(one_expert, start_sum, (w_gate, w_up, w_down, holder, weight_at))
    return summed[:TOKENS].astype(jnp.bfloat16)
```

```python
import functools

import jax
import jax.numpy as jnp
from jax import lax
from jax.experimental import pallas as pl
from jax.experimental.pallas import tpu as pltpu
from jax.sharding import PartitionSpec as P

BF = jnp.bfloat16
F32 = jnp.float32
NEAR = 8
FAR = 4
VM = pl.BlockSpec(memory_space=pltpu.VMEM)


def call(kernel, outs, name, limit=48 << 20, flops=0, moved=0, smem=False):
    def run(*args):
        specs = [VM] * len(args)
        if smem:
            specs[0] = pl.BlockSpec(memory_space=pltpu.SMEM)
        return pl.pallas_call(
            kernel,
            out_shape=[jax.ShapeDtypeStruct(s, t) for s, t in outs],
            in_specs=specs,
            out_specs=[VM] * len(outs),
            compiler_params=pltpu.CompilerParams(vmem_limit_bytes=limit),
            cost_estimate=pl.CostEstimate(flops=flops, bytes_accessed=moved, transcendentals=0),
            name=name,
        )(*args)

    return run


def dot(a, b):
    return jnp.dot(a, b, preferred_element_type=F32)


def dot_t(a, b):
    return lax.dot_general(a, b, (((0,), (0,)), ((), ())), preferred_element_type=F32)


def pick_kernel(ids, probs, tokens, wire1, pick2, mix1, mix2):
    rows, fanout = ids.shape
    experts = wire1.shape[0] // NEAR
    label = lax.broadcasted_iota(jnp.int32, (rows, experts), 1)
    p = probs[...]
    shares = (p / jnp.sum(p, axis=1, keepdims=True)).astype(BF).astype(F32)
    named = jnp.zeros((rows, experts), F32)
    share = jnp.zeros((rows, experts), F32)
    for k in range(fanout):
        hit = ids[:, k : k + 1] == label
        named = jnp.where(hit, 1.0, named)
        share = jnp.where(hit, shares[:, k : k + 1], share)
    i0 = lax.broadcasted_iota(jnp.int32, (rows, rows), 0)
    i1 = lax.broadcasted_iota(jnp.int32, (rows, rows), 1)
    eye = (i0 == i1).astype(BF)
    earlier = (i0 < i1).astype(BF)
    named = named.astype(BF)
    named_t = dot_t(named, eye)
    before_t = dot_t(named, earlier)
    share_t = dot_t(share.astype(BF), eye)
    seat = jnp.where(named_t > 0.5, before_t, -1.0).astype(jnp.int32)

    def spread(values, count):
        return jnp.broadcast_to(values[:, None, :], (experts, count, rows)).reshape(
            experts * count, rows
        )

    place = lax.broadcasted_iota(jnp.int32, (experts * NEAR, rows), 0) % NEAR
    hit1 = spread(seat, NEAR) == place
    one1 = hit1.astype(F32).astype(BF)
    mix1[...] = jnp.where(hit1, spread(share_t, NEAR), 0.0).astype(BF)
    hit2 = spread(seat, 2 * FAR) == (place % FAR) + NEAR
    pick = hit2.astype(F32)
    mix = jnp.where(hit2, spread(share_t, 2 * FAR), 0.0)
    low = place < FAR
    pick2[:, :rows] = jnp.where(low, pick, 0.0).astype(BF)
    pick2[:, rows:] = jnp.where(low, 0.0, pick).astype(BF)
    mix2[:, :rows] = jnp.where(low, mix, 0.0).astype(BF)
    mix2[:, rows:] = jnp.where(low, 0.0, mix).astype(BF)
    wire1[...] = dot(one1, tokens[...]).astype(BF)


def wire2_kernel(pick2, t0, t1, t2, t3, wire2):
    rows, band = t0.shape
    low = pick2[:, :rows]
    high = pick2[:, rows:]
    wire2[:, :band] = (dot(low, t0[...]) + dot(high, t2[...])).astype(BF)
    wire2[:, band:] = (dot(low, t1[...]) + dot(high, t3[...])).astype(BF)


def order(count):
    half = count // 2
    i = lax.broadcasted_iota(jnp.int32, (count, count), 0)
    j = lax.broadcasted_iota(jnp.int32, (count, count), 1)
    r = i % half
    return (j == (r // FAR) * (2 * FAR) + (i // half) * FAR + r % FAR).astype(F32).astype(BF)


def expert_kernel(where, *refs):
    own1, sib1 = refs[0:4], refs[4:8]
    own2, sib2, wg, wu, wd = refs[8:13]
    keep1, give1, keep2, give2 = refs[13:17]
    yh, core = where[0], where[1]
    band = own1[0].shape[1]
    rows1 = own1[0].shape[0]
    rows2 = own2.shape[0] // 2
    step = 256

    def offset(k, parity):
        return pl.multiple_of((2 * (k % 4) + parity) * band, band)

    seq = order(own2.shape[0])
    a_own = dot(seq, own2[...]).astype(BF)
    a_sib = dot(seq, sib2[...]).astype(BF)

    def chunk(pieces):
        g = None
        for piece, at in pieces:
            pg = dot(piece, wg[pl.ds(at, band), :])
            pu = dot(piece, wu[pl.ds(at, band), :])
            g, u = (pg, pu) if g is None else (g + pg, u + pu)
        return (g / (1.0 + jnp.exp(-g)) * u).astype(BF)

    far = []
    for k in range(4):
        r = slice((k // 2) * rows2, (k // 2 + 1) * rows2)
        c = slice((k % 2) * band, (k % 2 + 1) * band)
        far.append((a_own[r, c], offset(yh + 4 - k, core)))
        far.append((a_sib[r, c], offset(yh + 4 - k, 1 - core)))
    h2 = chunk(far)
    for k in range(4):
        at = offset(yh + k, 1 - core)
        give2[k] = dot(h2, wd[:, pl.ds(at, band)]).astype(BF)
        at = offset(yh + k, core)
        keep2[k] = dot(h2, wd[:, pl.ds(at, band)]).astype(BF)
    for m in range(0, rows1, step):
        near = []
        for k in range(4):
            near.append((own1[k][m : m + step, :], offset(yh + 4 - k, core)))
            near.append((sib1[k][m : m + step, :], offset(yh + 4 - k, 1 - core)))
        h1 = chunk(near)
        for k in range(4):
            at = offset(yh + k, 1 - core)
            give1[k, m : m + step, :] = dot(h1, wd[:, pl.ds(at, band)]).astype(BF)
            at = offset(yh + k, core)
            keep1[k, m : m + step, :] = dot(h1, wd[:, pl.ds(at, band)]).astype(BF)


def far_sum_kernel(keep2, give2, wire):
    rows, band = keep2.shape[1:]
    seq = order(2 * rows)
    for col in range(2):
        parts = []
        for half in range(2):
            k = 2 * half + col
            s = keep2[k].astype(F32) + give2[k].astype(F32)
            parts.append(s.astype(BF))
        both = jnp.concatenate(parts, axis=0)
        wire[:, col * band : (col + 1) * band] = dot_t(seq, both).astype(BF)


def far_mix_kernel(mix2, home, out):
    rows = out.shape[1]
    band = out.shape[2]
    for k in range(4):
        half, col = k // 2, k % 2
        out[k] = dot_t(
            mix2[:, half * rows : (half + 1) * rows], home[:, col * band : (col + 1) * band]
        ).astype(BF)


def last_kernel(mix1, home, f0, f1, f2, f3, out):
    total = dot_t(mix1[...], home[...])
    for f in (f0, f1, f2, f3):
        total = total + f[...].astype(F32)
    out[...] = total.astype(BF)


def body(tokens, expert_ids, router_probs, w_gate, w_up, w_down):
    rows, band = tokens.shape
    owners = lax.axis_size("expert")
    groups = lax.axis_size("dp")
    experts = owners
    features = w_gate.shape[1]
    seats1, seats2 = experts * NEAR, experts * FAR
    me = lax.axis_index("dp")
    where = jnp.stack([me // 2, me % 2]).astype(jnp.int32)

    def shift(x, k):
        return lax.ppermute(x, "dp", [(i, (i + 2 * k) % groups) for i in range(groups)])

    def swap(x):
        return lax.ppermute(x, "dp", [(i, i ^ 1) for i in range(groups)])

    def trade(x):
        x = x.reshape(experts, x.shape[0] // experts, x.shape[1])
        x = lax.all_to_all(x, "expert", split_axis=0, concat_axis=0, tiled=True)
        return x.reshape(-1, x.shape[2])

    bands = [tokens] + [shift(tokens, k) for k in (1, 2, 3)]
    wire1, pick2, mix1, mix2 = call(
        pick_kernel,
        [((seats1, band), BF), ((seats1, 2 * rows), BF), ((seats1, rows), BF), ((seats1, 2 * rows), BF)],
        "pick",
    )(expert_ids, router_probs, tokens)
    got1 = trade(wire1)
    (wire2,) = call(wire2_kernel, [((seats1, 2 * band), BF)], "wire2")(pick2, *bands)
    got2 = trade(wire2)
    own1 = [got1] + [shift(got1, k) for k in (1, 2, 3)]
    sib1 = [swap(x) for x in own1]
    sib2 = swap(got2)
    keep1, give1, keep2, give2 = call(
        expert_kernel,
        [
            ((4, seats1, band), BF),
            ((4, seats1, band), BF),
            ((4, seats2, band), BF),
            ((4, seats2, band), BF),
        ],
        "expert",
        smem=True,
        flops=6 * (seats1 + seats2) * features * w_gate.shape[2],
        moved=12 << 20,
    )(where, *own1, *sib1, got2, sib2, w_gate[0], w_up[0], w_down[0])
    give2 = swap(give2)
    give1 = swap(give1)
    (back2,) = call(far_sum_kernel, [((seats1, 2 * band), BF)], "far_sum")(keep2, give2)
    home2 = trade(back2)
    pair1 = [(keep1[k].astype(F32) + give1[k].astype(F32)) for k in range(4)]
    sent = [shift(pair1[k].astype(BF), k) for k in (1, 2, 3)]
    back1 = pair1[0]
    for s in sent:
        back1 = back1 + s.astype(F32)
    home1 = trade(back1.astype(BF))
    (part2,) = call(far_mix_kernel, [((4, rows, band), BF)], "far_mix")(mix2, home2)
    fars = [part2[0]] + [shift(part2[k], k) for k in (1, 2, 3)]
    (out,) = call(last_kernel, [((rows, band), BF)], "last")(mix1, home1, *fars)
    return out


def solution(mesh):
    return jax.shard_map(
        body,
        mesh=mesh,
        in_specs=(
            P("expert", "dp"),
            P("expert", None),
            P("expert", None),
            P("expert", None, "dp"),
            P("expert", None, "dp"),
            P("expert", "dp", None),
        ),
        out_specs=P("expert", "dp"),
        check_vma=False,
    )
```

```python
import jax
import jax.numpy as jnp
from jax import lax
from jax.experimental import pallas as pl
from jax.experimental.pallas import tpu as pltpu
from jax.sharding import PartitionSpec as P

BF = jnp.bfloat16
F32 = jnp.float32
NEAR = 8
FAR = 4
ROWS = 16
BANDS = 4
VM = pl.BlockSpec(memory_space=pltpu.VMEM)
SM = pl.BlockSpec(memory_space=pltpu.SMEM)


ANY = pl.BlockSpec(memory_space=pl.ANY)


def call(kernel, outs, name, specs, limit=8 << 20, flops=0, moved=0, scratch=()):
    return pl.pallas_call(
        kernel,
        out_shape=[jax.ShapeDtypeStruct(s, t) for s, t in outs],
        in_specs=specs,
        out_specs=[VM] * len(outs),
        scratch_shapes=list(scratch),
        compiler_params=pltpu.CompilerParams(vmem_limit_bytes=limit),
        cost_estimate=pl.CostEstimate(flops=flops, bytes_accessed=moved, transcendentals=0),
        name=name,
    )


def dot(a, b):
    return jnp.dot(a, b, preferred_element_type=F32)


def dot_t(a, b):
    return lax.dot_general(a, b, (((0,), (0,)), ((), ())), preferred_element_type=F32)


def pick_kernel(ids, probs, pick, mix):
    fanout, rows = ids.shape
    experts = pick.shape[0] // ROWS
    label = lax.broadcasted_iota(jnp.int32, (experts, rows), 0)
    p = probs[...]
    shares = (p / jnp.sum(p, axis=0, keepdims=True)).astype(BF).astype(F32)
    named = jnp.zeros((experts, rows), F32)
    share = jnp.zeros((experts, rows), F32)
    for k in range(fanout):
        hit = ids[k : k + 1, :] == label
        named = jnp.where(hit, 1.0, named)
        share = jnp.where(hit, shares[k : k + 1, :], share)
    i0 = lax.broadcasted_iota(jnp.int32, (rows, rows), 0)
    i1 = lax.broadcasted_iota(jnp.int32, (rows, rows), 1)
    before = dot(named.astype(BF), (i0 < i1).astype(F32).astype(BF))
    seat = jnp.where(named > 0.5, before, -1.0).astype(jnp.int32)

    def spread(values):
        return jnp.broadcast_to(values[:, None, :], (experts, ROWS, rows)).reshape(-1, rows)

    place = lax.broadcasted_iota(jnp.int32, (experts * ROWS, rows), 0) % ROWS
    seats = spread(seat)
    weights = spread(share)
    wanted = (
        place,
        place - NEAR,
        jnp.where((place >= NEAR) & (place < NEAR + FAR), place, 99),
        jnp.where(place >= NEAR + FAR, place - FAR, 99),
    )
    for i, want in enumerate(wanted):
        hit = seats == want
        if i == 0:
            hit = hit & (place < NEAR)
        elif i == 1:
            hit = hit & (want >= 0)
        pick[:, i * rows : (i + 1) * rows] = hit.astype(F32).astype(BF)
        mix[:, i * rows : (i + 1) * rows] = jnp.where(hit, weights, 0.0).astype(BF)


def wire_kernel(pick, toks, wire):
    rows, band = toks.shape[1:]
    low = pick[:, :rows]
    both = pick[:, : 2 * rows]
    far = pick[:, 2 * rows :]

    def pair(a, b):
        return jnp.concatenate([toks[a], toks[b]], axis=0)

    wire[:, :band] = dot(both, pair(0, 3)).astype(BF)
    wire[:, band : 2 * band] = (dot(low, toks[1]) + dot(far, pair(0, 2))).astype(BF)
    wire[:, 2 * band :] = (dot(low, toks[2]) + dot(far, pair(1, 3))).astype(BF)


def order(count):
    half = count // 2
    i = lax.broadcasted_iota(jnp.int32, (count, count), 0)
    j = lax.broadcasted_iota(jnp.int32, (count, count), 1)
    r = i % half
    return (j == (r // FAR) * (2 * FAR) + (i // half) * FAR + r % FAR).astype(F32).astype(BF)


def unpack(wire):
    band = wire.shape[1] // 3
    blocks = wire.shape[0] // ROWS
    tiles = wire[...].astype(F32).reshape(blocks, 2, NEAR, 3 * band)
    top = tiles[:, 0].reshape(blocks * NEAR, 3 * band).astype(BF)
    low = tiles[:, 1].reshape(blocks * NEAR, 3 * band).astype(BF)
    near = jnp.concatenate([top, low[:, :band]], axis=1)
    far = dot(order(blocks * NEAR), low[:, band:]).astype(BF)
    half = blocks * FAR
    far = jnp.concatenate([far[:half], far[half:]], axis=1)
    return near, far


def pack(near, far, wire):
    band = near.shape[1] // BANDS
    blocks = near.shape[0] // NEAR
    far = far.astype(BF)
    far = jnp.concatenate([far[:, : 2 * band], far[:, 2 * band :]], axis=0)
    far = dot_t(order(blocks * NEAR), far)
    low = jnp.concatenate([near[:, 3 * band :], far], axis=1)
    tiles = jnp.stack(
        [near[:, : 3 * band].reshape(blocks, NEAR, 3 * band), low.reshape(blocks, NEAR, 3 * band)],
        axis=1,
    )
    wire[...] = tiles.reshape(blocks * ROWS, 3 * band).astype(BF)


def fetch_pairs(parity, wg, wu, w, sems):
    band = w.shape[0] // BANDS
    wide = w.shape[1] // 2
    copies = []
    for k in range(BANDS):
        rows = pl.ds(pl.multiple_of((2 * k + parity) * band, band), band)
        for i, ref in enumerate((wg, wu)):
            copies.append(
                pltpu.make_async_copy(
                    ref.at[rows, :],
                    w.at[pl.ds(k * band, band), pl.ds(i * wide, wide)],
                    sems.at[2 * k + i],
                )
            )
    for c in copies:
        c.start()
    return copies


def first_kernel(where, own, wg, wu, acc, w, sems):
    copies = fetch_pairs(where[0], wg, wu, w, sems)
    near, far = unpack(own)
    n = near.shape[0]
    for c in copies:
        c.wait()
    acc[:n, :] = dot(near, w[...])
    acc[n:, :] = dot(far, w[...])


def fetch_down(parity, wd, w, sem):
    band = w.shape[1] // BANDS
    copies = []
    for k in range(BANDS):
        cols = pl.ds(pl.multiple_of((2 * k + parity) * band, band), band)
        copies.append(pltpu.make_async_copy(wd.at[:, cols], w.at[:, pl.ds(k * band, band)], sem.at[k]))
    for c in copies:
        c.start()
    return copies


def second_kernel(where, sib, acc, wg, wu, wd, h, give, w, wdown, sems, dsems):
    parity = 1 - where[0]
    copies = fetch_pairs(parity, wg, wu, w, sems)
    downs = fetch_down(parity, wd, wdown, dsems)
    near, far = unpack(sib)
    n = near.shape[0]
    wide = h.shape[1]
    for c in copies:
        c.wait()
    for x, at in ((near, slice(0, n)), (far, slice(n, acc.shape[0]))):
        both = acc[at, :] + dot(x, w[...])
        g, u = both[:, :wide], both[:, wide:]
        h[at, :] = (g / (1.0 + jnp.exp(-g)) * u).astype(BF)
    for c in downs:
        c.wait()
    pack(dot(h[:n, :], wdown[...]), dot(h[n:, :], wdown[...]), give)


def third_kernel(where, h, wd, keep, wdown, dsems):
    n = h.shape[0] // (NEAR + FAR) * NEAR
    for c in fetch_down(where[0], wd, wdown, dsems):
        c.wait()
    pack(dot(h[:n, :], wdown[...]), dot(h[n:, :], wdown[...]), keep)


def mix_kernel(mix, home, out):
    rows, band = out.shape[1:]
    parts = dot_t(mix[...], home[...])

    def at(i, j):
        return parts[i * rows : (i + 1) * rows, j * band : (j + 1) * band]

    out[0] = (at(0, 0) + at(2, 1)).astype(BF)
    out[1] = (at(0, 1) + at(2, 2)).astype(BF)
    out[2] = (at(0, 2) + at(3, 1)).astype(BF)
    out[3] = (at(1, 0) + at(3, 2)).astype(BF)


def body(tokens, expert_ids, router_probs, w_gate, w_up, w_down):
    rows, band = tokens.shape
    experts = lax.axis_size("expert")
    groups = lax.axis_size("dp")
    wide = w_gate.shape[2]
    seats = experts * (NEAR + FAR)
    core = lax.axis_index("dp") % 2
    where = core.astype(jnp.int32).reshape(1)
    lines = [list(range(c, groups, 2)) for c in range(2)]

    def swap(x):
        return lax.ppermute(x, "dp", [(i, i ^ 1) for i in range(groups)])

    def along(x):
        return lax.all_to_all(x, "dp", split_axis=0, concat_axis=0, tiled=True, axis_index_groups=lines)

    def trade(x):
        x = x.reshape(experts, ROWS, 3 * band)
        x = lax.all_to_all(x, "expert", split_axis=0, concat_axis=0, tiled=True)
        return x.reshape(experts * ROWS, 3 * band)

    toks = along(jnp.broadcast_to(tokens[None], (BANDS, rows, band)))
    square = ((experts * ROWS, BANDS * rows), BF)
    packed = ((experts * ROWS, 3 * band), BF)
    pick, mix = call(pick_kernel, [square, square], "pick", [VM, VM])(expert_ids.T, router_probs.T)
    (wire,) = call(wire_kernel, [packed], "wire", [VM, VM])(pick, toks)
    own = trade(wire)
    wg, wu, wd = w_gate[0], w_up[0], w_down[0]
    sib = swap(own)
    half = BANDS * band
    part = 2 * seats * half * wide
    pairs = [pltpu.VMEM((half, 2 * wide), BF)]
    downs = [pltpu.VMEM((wide, half), BF)]
    many, few = [pltpu.SemaphoreType.DMA((2 * BANDS,))], [pltpu.SemaphoreType.DMA((BANDS,))]
    (acc,) = call(
        first_kernel,
        [((seats, 2 * wide), F32)],
        "first",
        [SM, VM, ANY, ANY],
        limit=24 << 20,
        flops=2 * part,
        moved=6 << 20,
        scratch=pairs + many,
    )(where, own, wg, wu)
    h, give = call(
        second_kernel,
        [((seats, wide), BF), packed],
        "second",
        [SM, VM, VM, ANY, ANY, ANY],
        limit=24 << 20,
        flops=3 * part,
        moved=8 << 20,
        scratch=pairs + downs + many + few,
    )(where, sib, acc, wg, wu, wd)
    give = swap(give)
    (keep,) = call(
        third_kernel,
        [packed],
        "third",
        [SM, VM, ANY],
        limit=24 << 20,
        flops=part,
        moved=4 << 20,
        scratch=downs + few,
    )(where, h, wd)
    back = (keep.astype(F32) + give.astype(F32)).astype(BF)
    home = trade(back)
    (parts,) = call(mix_kernel, [((BANDS, rows, band), BF)], "mix", [VM, VM])(mix, home)
    parts = along(parts)
    return jnp.sum(parts.astype(F32), axis=0).astype(BF)


def solution(mesh):
    return jax.shard_map(
        body,
        mesh=mesh,
        in_specs=(
            P("expert", "dp"),
            P("expert", None),
            P("expert", None),
            P("expert", None, "dp"),
            P("expert", None, "dp"),
            P("expert", "dp", None),
        ),
        out_specs=P("expert", "dp"),
        check_vma=False,
    )
```

```python
import jax
import jax.numpy as jnp
from jax import lax
from jax.experimental import pallas as pl
from jax.experimental.pallas import tpu as pltpu
from jax.sharding import Mesh
from jax.sharding import PartitionSpec as P

BF = jnp.bfloat16
F32 = jnp.float32
NEAR = 8
FAR = 4
BANDS = 4
LIMIT = 32 << 20
FIRST_LIMIT = 47 << 20
DP = {"yh": 4, "core": 2}
EXPERT = {"z": 8, "yl": 2, "x": 4}
TRADE = ("yl", "z", "x")
VM = pl.BlockSpec(memory_space=pltpu.VMEM)
SM = pl.BlockSpec(memory_space=pltpu.SMEM)
ANY = pl.BlockSpec(memory_space=pl.ANY)


def call(kernel, outs, name, specs, limit=8 << 20, flops=0, moved=0, scratch=()):
    return pl.pallas_call(
        kernel,
        out_shape=[jax.ShapeDtypeStruct(s, t) for s, t in outs],
        in_specs=specs,
        out_specs=[VM] * len(outs),
        scratch_shapes=list(scratch),
        compiler_params=pltpu.CompilerParams(vmem_limit_bytes=limit),
        cost_estimate=pl.CostEstimate(flops=flops, bytes_accessed=moved, transcendentals=0),
        name=name,
    )


def dot(a, b):
    return jnp.dot(a, b, preferred_element_type=F32)


def dot_t(a, b):
    return lax.dot_general(a, b, (((0,), (0,)), ((), ())), preferred_element_type=F32)


def pick_kernel(ids, probs, pick, mix):
    fanout, rows = ids.shape
    experts = pick.shape[0] // NEAR
    at = lax.broadcasted_iota(jnp.int32, (experts, rows), 0)
    place = {}
    for axis in TRADE[::-1]:
        place[axis] = at % EXPERT[axis]
        at = at // EXPERT[axis]
    label = jnp.zeros((experts, rows), jnp.int32)
    for axis, size in EXPERT.items():
        label = label * size + place[axis]
    p = probs[...]
    shares = (p / jnp.sum(p, axis=0, keepdims=True)).astype(BF).astype(F32)
    named = jnp.zeros((experts, rows), F32)
    share = jnp.zeros((experts, rows), F32)
    for k in range(fanout):
        hit = ids[k : k + 1, :] == label
        named = jnp.where(hit, 1.0, named)
        share = jnp.where(hit, shares[k : k + 1, :], share)
    i0 = lax.broadcasted_iota(jnp.int32, (rows, rows), 0)
    i1 = lax.broadcasted_iota(jnp.int32, (rows, rows), 1)
    before = dot(named.astype(BF), (i0 < i1).astype(F32).astype(BF))
    seat = jnp.where(named > 0.5, before, -1.0).astype(jnp.int32)

    def spread(values):
        return jnp.broadcast_to(values[:, None, :], (experts, NEAR, rows)).reshape(-1, rows)

    place = lax.broadcasted_iota(jnp.int32, (experts * NEAR, rows), 0) % NEAR
    seats = spread(seat)
    weights = spread(share)
    far = seats == place % FAR + NEAR
    for i, hit in enumerate((seats == place, far & (place < FAR), far & (place >= FAR))):
        pick[:, i * rows : (i + 1) * rows] = hit.astype(F32).astype(BF)
        mix[:, i * rows : (i + 1) * rows] = jnp.where(hit, weights, 0.0).astype(BF)


def repeat_kernel(tokens, out):
    for k in range(BANDS):
        out[k] = tokens[...]


def wire_kernel(pick, toks, wire):
    rows, band = toks.shape[1:]
    for k in range(BANDS):
        wire[:, k * band : (k + 1) * band] = dot(pick[:, :rows], toks[k]).astype(BF)
    for j in range(2):
        both = jnp.concatenate([toks[j], toks[2 + j]], axis=0)
        at = (BANDS + j) * band
        wire[:, at : at + band] = dot(pick[:, rows:], both).astype(BF)


def order(count):
    half = count // 2
    i = lax.broadcasted_iota(jnp.int32, (count, count), 0)
    j = lax.broadcasted_iota(jnp.int32, (count, count), 1)
    r = i % half
    return (j == (r // FAR) * (2 * FAR) + (i // half) * FAR + r % FAR).astype(F32).astype(BF)


def far_rows(wire):
    count = wire.shape[0]
    x = dot(order(count), wire[:, wire.shape[1] // 3 * 2 :]).astype(BF)
    return jnp.concatenate([x[: count // 2], x[count // 2 :]], axis=1)


def fill(h, down, wire):
    count, width = wire.shape
    half = width // 3 * 2
    band = half // BANDS
    far = []
    for k in range(BANDS):
        cols = slice(k * band, (k + 1) * band)
        wire[:, cols] = dot(h[:count, :], down[:, cols]).astype(BF)
        far.append(dot(h[count:, :], down[:, cols]).astype(BF))
    top = jnp.concatenate(far[:2], axis=1)
    low = jnp.concatenate(far[2:], axis=1)
    wire[:, half:] = dot_t(order(count), jnp.concatenate([top, low], axis=0)).astype(BF)


def first_kernel(where, own, wg, wu, wd, acc_near, acc_far, up_sib, down_sib, down_own, up_own, sems):
    band = up_own.shape[0] // BANDS
    wide = wg.shape[1]
    copies = []

    def copy(src, dst):
        copies.append(pltpu.make_async_copy(src, dst, sems.at[len(copies)]))
        copies[-1].start()

    sides = ((up_own, down_own, where[0]), (up_sib, down_sib, 1 - where[0]))
    for up, _, parity in sides:
        for k in range(BANDS):
            at = pl.ds(pl.multiple_of((2 * k + parity) * band, band), band)
            to = pl.ds(k * band, band)
            copy(wg.at[at, :], up.at[to, pl.ds(0, wide)])
            copy(wu.at[at, :], up.at[to, pl.ds(wide, wide)])
    for _, down, parity in sides[::-1]:
        for k in range(BANDS):
            at = pl.ds(pl.multiple_of((2 * k + parity) * band, band), band)
            copy(wd.at[:, at], down.at[:, pl.ds(k * band, band)])
    far = far_rows(own)
    for c in copies[: 2 * BANDS]:
        c.wait()
    acc_near[...] = dot(own[:, : BANDS * band], up_own[...])
    acc_far[...] = dot(far, up_own[...])
    for c in copies[2 * BANDS :]:
        c.wait()


def second_kernel(sib, acc_near, acc_far, up, down, h, give):
    count = sib.shape[0]
    wide = h.shape[1]
    parts = (
        (acc_near, lambda: sib[:, : sib.shape[1] // 3 * 2], slice(0, count)),
        (acc_far, lambda: far_rows(sib), slice(count, h.shape[0])),
    )
    for acc, rows, at in parts:
        both = acc[...] + dot(rows(), up[...])
        g, u = both[:, :wide], both[:, wide:]
        h[at, :] = (g / (1.0 + jnp.exp(-g)) * u).astype(BF)
    fill(h, down, give)


def third_kernel(h, down, keep):
    fill(h, down, keep)


def mix_kernel(mix, home, out):
    rows, band = out.shape[1:]
    near = dot_t(mix[:, :rows], home[:, : BANDS * band])
    far = dot_t(mix[:, rows:], home[:, BANDS * band :])
    for k in range(BANDS):
        half, col = k // 2, k % 2
        a = near[:, k * band : (k + 1) * band]
        b = far[half * rows : (half + 1) * rows, col * band : (col + 1) * band]
        out[k] = (a + b).astype(BF)


def body(tokens, expert_ids, router_probs, w_gate, w_up, w_down):
    rows, band = tokens.shape
    experts = lax.axis_size(TRADE)
    wide = w_gate.shape[2]
    half = BANDS * band
    lines = experts * NEAR
    where = lax.axis_index("core").astype(jnp.int32).reshape(1)

    def swap(x):
        return lax.ppermute(x, "core", [(0, 1), (1, 0)])

    def along(x):
        return lax.all_to_all(x, "yh", split_axis=0, concat_axis=0, tiled=True)

    def trade(x):
        y = x.reshape(experts, NEAR, x.shape[1])
        y = lax.all_to_all(y, TRADE, split_axis=0, concat_axis=0, tiled=True)
        return y.reshape(x.shape)

    bands = ((BANDS, rows, band), BF)
    lists = ((lines, 3 * rows), BF)
    packed = ((lines, half // 2 * 3), BF)
    (toks,) = call(repeat_kernel, [bands], "repeat", [VM], limit=58 << 20)(tokens)
    toks = along(toks)
    pick, mix = call(pick_kernel, [lists, lists], "pick", [VM] * 2)(expert_ids.T, router_probs.T)
    (wire,) = call(wire_kernel, [packed], "wire", [VM] * 2)(pick, toks)
    own = trade(wire)
    sib = swap(own)
    part = 2 * experts * (NEAR + FAR) * half * wide
    sums = [((experts * n, 2 * wide), F32) for n in (NEAR, FAR)]
    ups, downs = ((half, 2 * wide), BF), ((wide, half), BF)
    acc_near, acc_far, up_sib, down_sib, down_own = call(
        first_kernel,
        sums + [ups, downs, downs],
        "first",
        [SM, VM, ANY, ANY, ANY],
        limit=FIRST_LIMIT,
        flops=2 * part,
        moved=6 << 20,
        scratch=[pltpu.VMEM(*ups), pltpu.SemaphoreType.DMA((6 * BANDS,))],
    )(where, own, w_gate[0], w_up[0], w_down[0])
    h, give = call(
        second_kernel,
        [((experts * (NEAR + FAR), wide), BF), packed],
        "second",
        [VM] * 5,
        limit=LIMIT,
        flops=3 * part,
        moved=8 << 20,
    )(sib, acc_near, acc_far, up_sib, down_sib)
    give = swap(give)
    (keep,) = call(third_kernel, [packed], "third", [VM] * 2, limit=LIMIT, flops=part, moved=4 << 20)(
        h, down_own
    )
    home = trade((keep.astype(F32) + give.astype(F32)).astype(BF))
    (parts,) = call(mix_kernel, [bands], "mix", [VM] * 2)(mix, home)
    return jnp.sum(along(parts).astype(F32), axis=0).astype(BF)


def solution(mesh):
    sizes = DP | EXPERT
    mesh = Mesh(mesh.devices.reshape(*sizes.values()), tuple(sizes))
    dp, expert = tuple(DP), tuple(EXPERT)
    return jax.shard_map(
        body,
        mesh=mesh,
        in_specs=(
            P(expert, dp),
            P(expert, None),
            P(expert, None),
            P(expert, None, dp),
            P(expert, None, dp),
            P(expert, dp, None),
        ),
        out_specs=P(expert, dp),
        check_vma=False,
    )
```

```python
import jax
import jax.numpy as jnp
from jax import lax
from jax.experimental import pallas as pl
from jax.experimental.pallas import tpu as pltpu
from jax.sharding import Mesh
from jax.sharding import PartitionSpec as P

BF = jnp.bfloat16
F32 = jnp.float32
NEAR = 8
FAR = 4
SEATS = NEAR + FAR
LINE = 4
LONG = 40_000_000_000
SHORT = 2_000_000_000
PLUS_LIMIT = 50 << 20
LOAD_LIMIT = 49 << 20
REST_LIMIT = 50 << 20
LIMIT = 32 << 20
PICK_LIMIT = 58 << 20
DP = {"yh": 4, "core": 2}
EXPERT = {"z": 8, "yl": 2, "x": 4}
TRADE = ("yl", "z", "x")
VM = pl.BlockSpec(memory_space=pltpu.VMEM)
SM = pl.BlockSpec(memory_space=pltpu.SMEM)
ANY = pl.BlockSpec(memory_space=pl.ANY)
HBM = pl.BlockSpec(memory_space=pltpu.HBM)


def call(kernel, outs, name, specs, limit=LIMIT, flops=0, moved=0, scratch=(), out_specs=None):
    return pl.pallas_call(
        kernel,
        out_shape=[jax.ShapeDtypeStruct(s, t) for s, t in outs],
        in_specs=specs,
        out_specs=out_specs or [VM] * len(outs),
        scratch_shapes=list(scratch),
        compiler_params=pltpu.CompilerParams(vmem_limit_bytes=limit),
        cost_estimate=pl.CostEstimate(flops=flops, bytes_accessed=moved, transcendentals=0),
        name=name,
    )


def dot(a, b):
    return jnp.dot(a, b, preferred_element_type=F32)


def dot_t(a, b):
    return lax.dot_general(a, b, (((0,), (0,)), ((), ())), preferred_element_type=F32)


def fill(pick, tokens, wire):
    rows, band = tokens.shape
    t = tokens[...]
    wire[:, :band] = dot(pick[:, :rows], t).astype(BF)
    halves = jnp.concatenate([t[:, : band // 2], t[:, band // 2 :]], axis=0)
    wire[:, band:] = dot(pick[:, rows:], halves).astype(BF)


def pick_kernel(ids, probs, tokens, wire, pick, mix):
    fanout, rows = ids.shape
    experts = pick.shape[0] // NEAR
    at = lax.broadcasted_iota(jnp.int32, (experts, rows), 0)
    place = {}
    for axis in TRADE[::-1]:
        place[axis] = at % EXPERT[axis]
        at = at // EXPERT[axis]
    label = jnp.zeros((experts, rows), jnp.int32)
    for axis, size in EXPERT.items():
        label = label * size + place[axis]
    p = probs[...]
    shares = (p / jnp.sum(p, axis=0, keepdims=True)).astype(BF).astype(F32)
    named = jnp.zeros((experts, rows), F32)
    share = jnp.zeros((experts, rows), F32)
    for k in range(fanout):
        hit = ids[k : k + 1, :] == label
        named = jnp.where(hit, 1.0, named)
        share = jnp.where(hit, shares[k : k + 1, :], share)
    i0 = lax.broadcasted_iota(jnp.int32, (rows, rows), 0)
    i1 = lax.broadcasted_iota(jnp.int32, (rows, rows), 1)
    before = dot(named.astype(BF), (i0 < i1).astype(F32).astype(BF))
    seat = jnp.where(named > 0.5, before, -1.0).astype(jnp.int32)

    def spread(values):
        return jnp.broadcast_to(values[:, None, :], (experts, NEAR, rows)).reshape(-1, rows)

    place = lax.broadcasted_iota(jnp.int32, (experts * NEAR, rows), 0) % NEAR
    seats = spread(seat)
    weights = spread(share)
    far = seats == place % FAR + NEAR
    for i, hit in enumerate((seats == place, far & (place < FAR), far & (place >= FAR))):
        pick[:, i * rows : (i + 1) * rows] = hit.astype(F32).astype(BF)
        mix[:, i * rows : (i + 1) * rows] = jnp.where(hit, weights, 0.0).astype(BF)
    fill(pick, tokens, wire)


def order(count):
    half = count // 2
    i = lax.broadcasted_iota(jnp.int32, (count, count), 0)
    j = lax.broadcasted_iota(jnp.int32, (count, count), 1)
    r = i % half
    return (j == (r // FAR) * (2 * FAR) + (i // half) * FAR + r % FAR).astype(F32).astype(BF)


def spread_far(far, wide):
    half = far.shape[0] // 2
    parts = []
    for i in range(far.shape[1] // wide):
        cols = slice(i * wide, (i + 1) * wide)
        parts += [far[:half, cols], far[half:, cols]]
    return jnp.concatenate(parts, axis=1)


def unpack(wires):
    count, width = wires[0].shape
    band = width // 3 * 2
    near = jnp.concatenate([w[:, :band] for w in wires], axis=1)
    far = jnp.concatenate([w[:, band:] for w in wires], axis=1)
    far = dot(order(count), far).astype(BF)
    return near, spread_far(far, band // 2)


def pack(near, far, down, wires):
    count, width = wires[0].shape
    band = width // 3 * 2
    wide = band // 2
    top, low = [], []
    for i, wire in enumerate(wires):
        cols = slice(i * band, (i + 1) * band)
        wire[:, :band] = dot(near, down[:, cols]).astype(BF)
        part = dot(far, down[:, cols]).astype(BF)
        top.append(part[:, :wide])
        low.append(part[:, wide:])
    both = jnp.concatenate([jnp.concatenate(top, axis=1), jnp.concatenate(low, axis=1)], axis=0)
    both = dot_t(order(count), both).astype(BF)
    for i, wire in enumerate(wires):
        wire[:, band:] = both[:, i * wide : (i + 1) * wide]


def band_at(k, parity, band):
    return pl.ds(pl.multiple_of((2 * (k % LINE) + parity) * band, band), band)


class Fetch:
    def __init__(self, sems):
        self.sems, self.copies = sems, []

    def __call__(self, src, dst):
        self.copies.append(pltpu.make_async_copy(src, dst, self.sems.at[len(self.copies)]))
        self.copies[-1].start()

    def up(self, wg, wu, dst, slot, rows):
        wide, band = wg.shape[1], rows.size
        to = pl.ds(slot * band, band)
        self(wg.at[rows, :], dst.at[to, pl.ds(0, wide)])
        self(wu.at[rows, :], dst.at[to, pl.ds(wide, wide)])

    def wait(self, first=0, last=None):
        for c in self.copies[first:last]:
            c.wait()


def place():
    return lax.axis_index("yh"), lax.axis_index("core")


def plus_kernel(wg, wu, *refs):
    wires, (out_near, out_far, up, x, y, near_sum, far_sum, sems) = refs[:6], refs[6:]
    yh, core = place()
    count, width = wires[0].shape
    band = up.shape[0] // 6
    wide = band // 2
    fetch = Fetch(sems)
    for i, wire in enumerate(wires):
        fetch(wire.at[:, pl.ds(band, wide)], y.at[:, pl.ds(i * wide, wide)])
    for i, wire in enumerate(wires):
        fetch(wire.at[:, pl.ds(0, band)], x.at[:, pl.ds(i * band, band)])
    for slot, (k, parity) in enumerate((k, p) for k in (0, 1, 3) for p in (core, 1 - core)):
        fetch.up(wg, wu, up, slot, band_at(yh + LINE - k, parity, band))
    seq = order(count)
    fetch.wait(0, 6)
    far = spread_far(dot(seq, y[...]).astype(BF), wide)
    fetch.wait(6)
    near_sum[...] = dot(x[...], up[...])
    back = Fetch(sems)
    back(near_sum, out_near)
    far_sum[...] = dot(far, up[...])
    back(far_sum, out_far)
    back.wait()


def load_kernel(wg, wu, wd, acc_near, acc_far, out_top, out_low, out_far, up, give13, sems):
    yh, core = place()
    band = up.shape[0] // 2
    fetch = Fetch(sems)
    half = out_top.shape[0]
    fetch(acc_near.at[pl.ds(0, half), :], out_top)
    fetch(acc_near.at[pl.ds(half, half), :], out_low)
    fetch(acc_far, out_far)
    fetch.up(wg, wu, up, 0, band_at(yh + 2, core, band))
    fetch.up(wg, wu, up, 1, band_at(yh + 2, 1 - core, band))
    for slot, k in enumerate((1, 3)):
        fetch(wd.at[:, band_at(yh + k, 1 - core, band)], give13.at[:, pl.ds(slot * band, band)])
    fetch.wait()


def halves(ref):
    rows = ref.shape[0] // 2
    return [ref.at[pl.ds(i * rows, rows), :] for i in range(2)]


def hidden_kernel(own, sib, acc_top, acc_low, acc_far, up, down, h, give):
    near, far = unpack((own, sib))
    n = near.shape[0]
    wide = h.shape[1]
    half = n // 2
    parts = (
        (near[:half], acc_top, slice(0, half)),
        (near[half:], acc_low, slice(half, n)),
        (far, acc_far, slice(n, h.shape[0])),
    )
    for x, acc, at in parts:
        both = acc[...] + dot(x, up[...])
        g, u = both[:, :wide], both[:, wide:]
        h[at, :] = (g / (1.0 + jnp.exp(-g)) * u).astype(BF)
    pack(h[:n, :], h[n:, :], down, halves(give))


def rest_kernel(h, wd, give, keep1, keep3, keep2, keep0, give20, keep13, keep20, sems):
    yh, core = place()
    band = give20.shape[1] // 2
    fetch = Fetch(sems)
    for down, ks, parity in ((give20, (2, 0), 1 - core), (keep13, (1, 3), core), (keep20, (2, 0), core)):
        for slot, k in enumerate(ks):
            fetch(wd.at[:, band_at(yh + k, parity, band)], down.at[:, pl.ds(slot * band, band)])
    n = h.shape[0] // SEATS * NEAR
    near, far = h[:n, :], h[n:, :]
    fetch.wait()
    pack(near, far, keep13, (keep1, keep3))
    pack(near, far, give20, halves(give))
    pack(near, far, keep20, (keep2, keep0))


def pair_kernel(keep1, keep3, give, one, three):
    for a, b, out in zip((keep1, keep3), halves(give), (one, three)):
        out[...] = (a[...].astype(F32) + b[...].astype(F32)).astype(BF)


def sum_kernel(keep0, give, one, three, out):
    total = keep0[...].astype(F32) + halves(give)[1][...].astype(F32)
    out[...] = (total + one[...].astype(F32) + three[...].astype(F32)).astype(BF)


def two_sum_kernel(keep2, give, out):
    out[...] = (keep2[...].astype(F32) + halves(give)[0][...].astype(F32)).astype(BF)


def mixed(mix, home):
    rows = mix.shape[1] // 3
    band = home.shape[1] // 3 * 2
    total = dot_t(mix[:, :rows], home[:, :band])
    rest = dot_t(mix[:, rows:], home[:, band:])
    return total + jnp.concatenate([rest[:rows], rest[rows:]], axis=1)


def mix_kernel(mix, home, out):
    out[...] = mixed(mix, home).astype(BF)


def last_kernel(mix, home, other, out):
    out[...] = (mixed(mix, home) + other[...].astype(F32)).astype(BF)


def body(tokens, expert_ids, router_probs, w_gate, w_up, w_down):
    rows, band = tokens.shape
    experts = lax.axis_size(TRADE)
    wide = w_gate.shape[2]
    lines = experts * NEAR

    def swap(x):
        return lax.ppermute(x, "core", [(0, 1), (1, 0)])

    def shift(x, k):
        return lax.ppermute(x, "yh", [(i, (i + k) % LINE) for i in range(LINE)])

    def trade(x):
        y = x.reshape(experts, NEAR, x.shape[1])
        y = lax.all_to_all(y, TRADE, split_axis=0, concat_axis=0, tiled=True)
        return y.reshape(x.shape)

    tie = lax.optimization_barrier
    wg, wu, wd = w_gate[0], w_up[0], w_down[0]
    width = band // 2 * 3
    wire, two = ((lines, width), BF), ((2 * lines, width), BF)
    sums = [((experts * n, 2 * wide), F32) for n in (NEAR, FAR)]
    lists = ((lines, 3 * rows), BF)
    work = 2 * experts * SEATS * band * wide
    sems = lambda n: pltpu.SemaphoreType.DMA((n,))
    other = shift(tokens, 2)
    wire0, pick, mix = call(pick_kernel, [wire, lists, lists], "pick", [VM] * 3, limit=PICK_LIMIT)(
        expert_ids.T, router_probs.T, tokens
    )
    got0 = trade(wire0)
    (wire2,) = call(fill, [wire], "wire", [VM] * 2)(pick, other)
    got0, wire2 = tie((got0, wire2))
    got1, got3 = shift(got0, 1), shift(got0, 3)
    got2 = trade(wire2)
    sib0, sib1, sib3 = swap(got0), swap(got1), swap(got3)
    sums0 = call(
        plus_kernel,
        sums,
        "plus",
        [ANY] * 8,
        limit=PLUS_LIMIT,
        flops=SHORT,
        scratch=[
            pltpu.VMEM((6 * band, 2 * wide), BF),
            pltpu.VMEM((lines, 6 * band), BF),
            pltpu.VMEM((lines, 3 * band), BF),
        ]
        + [pltpu.VMEM(*x) for x in sums]
        + [sems(24)],
        out_specs=[HBM] * 2,
    )(wg, wu, got0, sib0, got1, sib1, got3, sib3)
    got2, sums0 = tie((got2, sums0))
    sib2 = swap(got2)
    pair = ((wide, 2 * band), BF)
    top, low, far, up2, give13 = call(
        load_kernel,
        [((experts * FAR, 2 * wide), F32)] * 3 + [((2 * band, 2 * wide), BF), pair],
        "load",
        [ANY, ANY, ANY, HBM, HBM],
        limit=LOAD_LIMIT,
        scratch=[sems(9)],
    )(wg, wu, wd, *sums0)
    h, give_a = call(
        hidden_kernel, [((experts * SEATS, wide), BF), two], "hidden", [VM] * 7, flops=6 * work
    )(got2, sib2, top, low, far, up2, give13)
    give_a = swap(give_a)
    give_b, keep1, keep3, keep2, keep0 = call(
        rest_kernel,
        [two] + [wire] * 4,
        "rest",
        [VM, ANY],
        limit=REST_LIMIT,
        flops=6 * work,
        scratch=[pltpu.VMEM(*pair)] * 3 + [sems(6)],
    )(h, wd)
    one, three = call(pair_kernel, [wire] * 2, "pair", [VM] * 3)(keep1, keep3, give_a)
    one, three, give_b = tie((one, three, give_b))
    one, three = shift(one, 1), shift(three, 3)
    give_b = swap(give_b)
    (back2,) = call(two_sum_kernel, [wire], "two_sum", [VM] * 2)(keep2, give_b)
    home2 = trade(back2)
    (back0,) = call(sum_kernel, [wire], "sum", [VM] * 4, flops=LONG)(keep0, give_b, one, three)
    home0 = trade(back0)
    (part,) = call(mix_kernel, [((rows, band), BF)], "mix", [VM] * 2)(mix, home2)
    (out,) = call(last_kernel, [((rows, band), BF)], "last", [VM] * 3)(mix, home0, shift(part, 2))
    return out


def solution(mesh):
    sizes = DP | EXPERT
    mesh = Mesh(mesh.devices.reshape(*sizes.values()), tuple(sizes))
    dp, expert = tuple(DP), tuple(EXPERT)
    return jax.shard_map(
        body,
        mesh=mesh,
        in_specs=(
            P(expert, dp),
            P(expert, None),
            P(expert, None),
            P(expert, None, dp),
            P(expert, None, dp),
            P(expert, dp, None),
        ),
        out_specs=P(expert, dp),
        check_vma=False,
    )
```

```python
import jax
import jax.numpy as jnp
from jax import lax
from jax.experimental import pallas as pl
from jax.experimental.pallas import tpu as pltpu
from jax.sharding import Mesh
from jax.sharding import PartitionSpec as P

BF = jnp.bfloat16
F32 = jnp.float32
NEAR = 8
FAR = 4
SEATS = NEAR + FAR
LINE = 4
LONG = 40_000_000_000
SHORT = 2_000_000_000
PLUS_LIMIT = 50 << 20
LOAD_LIMIT = 48 << 20
REST_LIMIT = 32 << 20
LIMIT = 32 << 20
PICK_LIMIT = 62 << 20
DP = {"yh": 4, "core": 2}
EXPERT = {"z": 8, "yl": 2, "x": 4}
TRADE = ("yl", "z", "x")
VM = pl.BlockSpec(memory_space=pltpu.VMEM)
SM = pl.BlockSpec(memory_space=pltpu.SMEM)
ANY = pl.BlockSpec(memory_space=pl.ANY)
HBM = pl.BlockSpec(memory_space=pltpu.HBM)


def call(kernel, outs, name, specs, limit=LIMIT, flops=0, moved=0, scratch=(), out_specs=None):
    return pl.pallas_call(
        kernel,
        out_shape=[jax.ShapeDtypeStruct(s, t) for s, t in outs],
        in_specs=specs,
        out_specs=out_specs or [VM] * len(outs),
        scratch_shapes=list(scratch),
        compiler_params=pltpu.CompilerParams(vmem_limit_bytes=limit),
        cost_estimate=pl.CostEstimate(flops=flops, bytes_accessed=moved, transcendentals=0),
        name=name,
    )


def dot(a, b):
    return jnp.dot(a, b, preferred_element_type=F32)


def dot_t(a, b):
    return lax.dot_general(a, b, (((0,), (0,)), ((), ())), preferred_element_type=F32)


def fill(pick, tokens, wire):
    rows, band = tokens.shape
    t = tokens[...]
    wire[:, :band] = dot(pick[:, :rows], t).astype(BF)
    halves = jnp.concatenate([t[:, : band // 2], t[:, band // 2 :]], axis=0)
    wire[:, band:] = dot(pick[:, rows:], halves).astype(BF)


def pick_kernel(ids, probs, tokens, wire, pick, mix):
    fanout, rows = ids.shape
    experts = pick.shape[0] // NEAR
    at = lax.broadcasted_iota(jnp.int32, (experts, rows), 0)
    place = {}
    for axis in TRADE[::-1]:
        place[axis] = at % EXPERT[axis]
        at = at // EXPERT[axis]
    label = jnp.zeros((experts, rows), jnp.int32)
    for axis, size in EXPERT.items():
        label = label * size + place[axis]
    p = probs[...]
    shares = (p / jnp.sum(p, axis=0, keepdims=True)).astype(BF).astype(F32)
    named = jnp.zeros((experts, rows), F32)
    share = jnp.zeros((experts, rows), F32)
    for k in range(fanout):
        hit = ids[k : k + 1, :] == label
        named = jnp.where(hit, 1.0, named)
        share = jnp.where(hit, shares[k : k + 1, :], share)
    i0 = lax.broadcasted_iota(jnp.int32, (rows, rows), 0)
    i1 = lax.broadcasted_iota(jnp.int32, (rows, rows), 1)
    before = dot(named.astype(BF), (i0 < i1).astype(F32).astype(BF))
    seat = jnp.where(named > 0.5, before, -1.0).astype(jnp.int32)

    def spread(values):
        return jnp.broadcast_to(values[:, None, :], (experts, NEAR, rows)).reshape(-1, rows)

    place = lax.broadcasted_iota(jnp.int32, (experts * NEAR, rows), 0) % NEAR
    seats = spread(seat)
    weights = spread(share)
    far = seats == place % FAR + NEAR
    for i, hit in enumerate((seats == place, far & (place < FAR), far & (place >= FAR))):
        pick[:, i * rows : (i + 1) * rows] = hit.astype(F32).astype(BF)
        mix[:, i * rows : (i + 1) * rows] = jnp.where(hit, weights, 0.0).astype(BF)
    fill(pick, tokens, wire)


def order(count):
    half = count // 2
    i = lax.broadcasted_iota(jnp.int32, (count, count), 0)
    j = lax.broadcasted_iota(jnp.int32, (count, count), 1)
    r = i % half
    return (j == (r // FAR) * (2 * FAR) + (i // half) * FAR + r % FAR).astype(F32).astype(BF)


def spread_far(far, wide):
    half = far.shape[0] // 2
    parts = []
    for i in range(far.shape[1] // wide):
        cols = slice(i * wide, (i + 1) * wide)
        parts += [far[:half, cols], far[half:, cols]]
    return jnp.concatenate(parts, axis=1)


def unpack(wires):
    count, width = wires[0].shape
    band = width // 3 * 2
    near = jnp.concatenate([w[:, :band] for w in wires], axis=1)
    far = jnp.concatenate([w[:, band:] for w in wires], axis=1)
    far = dot(order(count), far).astype(BF)
    return near, spread_far(far, band // 2)


def pack(near, far, down, wires):
    count, width = wires[0].shape
    band = width // 3 * 2
    wide = band // 2
    top, low = [], []
    for i, wire in enumerate(wires):
        cols = slice(i * band, (i + 1) * band)
        wire[:, :band] = dot(near, down[:, cols]).astype(BF)
        part = dot(far, down[:, cols]).astype(BF)
        top.append(part[:, :wide])
        low.append(part[:, wide:])
    both = jnp.concatenate([jnp.concatenate(top, axis=1), jnp.concatenate(low, axis=1)], axis=0)
    both = dot_t(order(count), both).astype(BF)
    for i, wire in enumerate(wires):
        wire[:, band:] = both[:, i * wide : (i + 1) * wide]


def band_at(k, parity, band):
    return pl.ds(pl.multiple_of((2 * (k % LINE) + parity) * band, band), band)


class Fetch:
    def __init__(self, sems):
        self.sems, self.copies = sems, []

    def __call__(self, src, dst):
        self.copies.append(pltpu.make_async_copy(src, dst, self.sems.at[len(self.copies)]))
        self.copies[-1].start()

    def up(self, wg, wu, dst, slot, rows):
        wide, band = wg.shape[1], rows.size
        to = pl.ds(slot * band, band)
        self(wg.at[rows, :], dst.at[to, pl.ds(0, wide)])
        self(wu.at[rows, :], dst.at[to, pl.ds(wide, wide)])

    def wait(self, first=0, last=None):
        for c in self.copies[first:last]:
            c.wait()


def place():
    return lax.axis_index("yh"), lax.axis_index("core")


def plus_kernel(wg, wu, *refs):
    wires, (out_near, out_far, up, x, y, near_sum, far_sum, sems) = refs[:6], refs[6:]
    yh, core = place()
    count, width = wires[0].shape
    band = up.shape[0] // 6
    wide = band // 2
    fetch = Fetch(sems)
    for i, wire in enumerate(wires):
        fetch(wire.at[:, pl.ds(band, wide)], y.at[:, pl.ds(i * wide, wide)])
    for i, wire in enumerate(wires):
        fetch(wire.at[:, pl.ds(0, band)], x.at[:, pl.ds(i * band, band)])
    for slot, (k, parity) in enumerate((k, p) for k in (0, 1, 3) for p in (core, 1 - core)):
        fetch.up(wg, wu, up, slot, band_at(yh + LINE - k, parity, band))
    seq = order(count)
    fetch.wait(0, 6)
    far = spread_far(dot(seq, y[...]).astype(BF), wide)
    fetch.wait(6)
    near_sum[...] = dot(x[...], up[...])
    back = Fetch(sems)
    back(near_sum, out_near)
    far_sum[...] = dot(far, up[...])
    back(far_sum, out_far)
    back.wait()


def load_kernel(wg, wu, wd, acc_near, acc_far, out_top, out_low, out_far, up, give13, give20, keep13, keep20, sems):
    yh, core = place()
    band = up.shape[0] // 2
    fetch = Fetch(sems)
    half = out_top.shape[0]
    fetch(acc_near.at[pl.ds(0, half), :], out_top)
    fetch(acc_near.at[pl.ds(half, half), :], out_low)
    fetch(acc_far, out_far)
    fetch.up(wg, wu, up, 0, band_at(yh + 2, core, band))
    fetch.up(wg, wu, up, 1, band_at(yh + 2, 1 - core, band))
    downs = ((give13, (1, 3), 1 - core), (give20, (2, 0), 1 - core), (keep13, (1, 3), core), (keep20, (2, 0), core))
    for down, ks, parity in downs:
        for slot, k in enumerate(ks):
            fetch(wd.at[:, band_at(yh + k, parity, band)], down.at[:, pl.ds(slot * band, band)])
    fetch.wait()


def halves(ref):
    rows = ref.shape[0] // 2
    return [ref.at[pl.ds(i * rows, rows), :] for i in range(2)]


def hidden_kernel(own, sib, acc_top, acc_low, acc_far, up, down, h, give):
    near, far = unpack((own, sib))
    n = near.shape[0]
    wide = h.shape[1]
    half = n // 2
    parts = (
        (near[:half], acc_top, slice(0, half)),
        (near[half:], acc_low, slice(half, n)),
        (far, acc_far, slice(n, h.shape[0])),
    )
    for x, acc, at in parts:
        both = acc[...] + dot(x, up[...])
        g, u = both[:, :wide], both[:, wide:]
        h[at, :] = (g / (1.0 + jnp.exp(-g)) * u).astype(BF)
    pack(h[:n, :], h[n:, :], down, halves(give))


def rest_kernel(h, give20, keep13, keep20, give, keep1, keep3, keep2, keep0):
    n = h.shape[0] // SEATS * NEAR
    near, far = h[:n, :], h[n:, :]
    pack(near, far, keep13, (keep1, keep3))
    pack(near, far, give20, halves(give))
    pack(near, far, keep20, (keep2, keep0))


def pair_kernel(keep1, keep3, give, one, three):
    for a, b, out in zip((keep1, keep3), halves(give), (one, three)):
        out[...] = (a[...].astype(F32) + b[...].astype(F32)).astype(BF)


def sum_kernel(keep0, give, one, three, out):
    total = keep0[...].astype(F32) + halves(give)[1][...].astype(F32)
    out[...] = (total + one[...].astype(F32) + three[...].astype(F32)).astype(BF)


def two_sum_kernel(keep2, give, out):
    out[...] = (keep2[...].astype(F32) + halves(give)[0][...].astype(F32)).astype(BF)


def mixed(mix, home):
    rows = mix.shape[1] // 3
    band = home.shape[1] // 3 * 2
    total = dot_t(mix[:, :rows], home[:, :band])
    rest = dot_t(mix[:, rows:], home[:, band:])
    return total + jnp.concatenate([rest[:rows], rest[rows:]], axis=1)


def mix_kernel(mix, home, out):
    out[...] = mixed(mix, home).astype(BF)


def last_kernel(mix, home, other, out):
    out[...] = (mixed(mix, home) + other[...].astype(F32)).astype(BF)


def body(tokens, expert_ids, router_probs, w_gate, w_up, w_down):
    rows, band = tokens.shape
    experts = lax.axis_size(TRADE)
    wide = w_gate.shape[2]
    lines = experts * NEAR

    def swap(x):
        return lax.ppermute(x, "core", [(0, 1), (1, 0)])

    def shift(x, k):
        return lax.ppermute(x, "yh", [(i, (i + k) % LINE) for i in range(LINE)])

    def trade(x):
        y = x.reshape(experts, NEAR, x.shape[1])
        y = lax.all_to_all(y, TRADE, split_axis=0, concat_axis=0, tiled=True)
        return y.reshape(x.shape)

    tie = lax.optimization_barrier
    wg, wu, wd = w_gate[0], w_up[0], w_down[0]
    width = band // 2 * 3
    wire, two = ((lines, width), BF), ((2 * lines, width), BF)
    sums = [((experts * n, 2 * wide), F32) for n in (NEAR, FAR)]
    lists = ((lines, 3 * rows), BF)
    work = 2 * experts * SEATS * band * wide
    sems = lambda n: pltpu.SemaphoreType.DMA((n,))
    other = shift(tokens, 2)
    wire0, pick, mix = call(pick_kernel, [wire, lists, lists], "pick", [VM] * 3, limit=PICK_LIMIT)(
        expert_ids.T, router_probs.T, tokens
    )
    got0 = trade(wire0)
    (wire2,) = call(fill, [wire], "wire", [VM] * 2)(pick, other)
    got0, wire2 = tie((got0, wire2))
    got1, got3 = shift(got0, 1), shift(got0, 3)
    got2 = trade(wire2)
    sib0, sib1, sib3 = swap(got0), swap(got1), swap(got3)
    sums0 = call(
        plus_kernel,
        sums,
        "plus",
        [ANY] * 8,
        limit=PLUS_LIMIT,
        flops=SHORT,
        scratch=[
            pltpu.VMEM((6 * band, 2 * wide), BF),
            pltpu.VMEM((lines, 6 * band), BF),
            pltpu.VMEM((lines, 3 * band), BF),
        ]
        + [pltpu.VMEM(*x) for x in sums]
        + [sems(24)],
        out_specs=[HBM] * 2,
    )(wg, wu, got0, sib0, got1, sib1, got3, sib3)
    got2, sums0 = tie((got2, sums0))
    sib2 = swap(got2)
    pair = ((wide, 2 * band), BF)
    top, low, far, up2, give13, give20, keep13, keep20 = call(
        load_kernel,
        [((experts * FAR, 2 * wide), F32)] * 3 + [((2 * band, 2 * wide), BF)] + [pair] * 4,
        "load",
        [ANY, ANY, ANY, HBM, HBM],
        limit=LOAD_LIMIT,
        scratch=[sems(15)],
    )(wg, wu, wd, *sums0)
    h, give_a = call(
        hidden_kernel, [((experts * SEATS, wide), BF), two], "hidden", [VM] * 7, flops=6 * work
    )(got2, sib2, top, low, far, up2, give13)
    give_a = swap(give_a)
    give_b, keep1, keep3, keep2, keep0 = call(
        rest_kernel,
        [two] + [wire] * 4,
        "rest",
        [VM] * 4,
        limit=REST_LIMIT,
        flops=6 * work,
    )(h, give20, keep13, keep20)
    one, three = call(pair_kernel, [wire] * 2, "pair", [VM] * 3)(keep1, keep3, give_a)
    one, three, give_b = tie((one, three, give_b))
    one, three = shift(one, 1), shift(three, 3)
    give_b = swap(give_b)
    (back2,) = call(two_sum_kernel, [wire], "two_sum", [VM] * 2)(keep2, give_b)
    home2 = trade(back2)
    (back0,) = call(sum_kernel, [wire], "sum", [VM] * 4, flops=LONG)(keep0, give_b, one, three)
    home0 = trade(back0)
    (part,) = call(mix_kernel, [((rows, band), BF)], "mix", [VM] * 2)(mix, home2)
    (out,) = call(last_kernel, [((rows, band), BF)], "last", [VM] * 3)(mix, home0, shift(part, 2))
    return out


def solution(mesh):
    sizes = DP | EXPERT
    mesh = Mesh(mesh.devices.reshape(*sizes.values()), tuple(sizes))
    dp, expert = tuple(DP), tuple(EXPERT)
    return jax.shard_map(
        body,
        mesh=mesh,
        in_specs=(
            P(expert, dp),
            P(expert, None),
            P(expert, None),
            P(expert, None, dp),
            P(expert, None, dp),
            P(expert, dp, None),
        ),
        out_specs=P(expert, dp),
        check_vma=False,
    )
```

```python
import jax
import jax.numpy as jnp
from jax import lax
from jax.experimental import pallas as pl
from jax.experimental.pallas import tpu as pltpu
from jax.sharding import Mesh
from jax.sharding import PartitionSpec as P

BF = jnp.bfloat16
F32 = jnp.float32
NEAR = 8
FAR = 4
SEATS = NEAR + FAR
LINE = 4
LONG = 40_000_000_000
SHORT = 2_000_000_000
PLUS_LIMIT = 50 << 20
LOAD_LIMIT = 48 << 20
REST_LIMIT = 32 << 20
LIMIT = 32 << 20
PICK_LIMIT = 62 << 20
DP = {"yh": 4, "core": 2}
EXPERT = {"z": 8, "yl": 2, "x": 4}
TRADE = ("yl", "z", "x")
VM = pl.BlockSpec(memory_space=pltpu.VMEM)
SM = pl.BlockSpec(memory_space=pltpu.SMEM)
ANY = pl.BlockSpec(memory_space=pl.ANY)
HBM = pl.BlockSpec(memory_space=pltpu.HBM)


def call(kernel, outs, name, specs, limit=LIMIT, flops=0, moved=0, scratch=(), out_specs=None):
    return pl.pallas_call(
        kernel,
        out_shape=[jax.ShapeDtypeStruct(s, t) for s, t in outs],
        in_specs=specs,
        out_specs=out_specs or [VM] * len(outs),
        scratch_shapes=list(scratch),
        compiler_params=pltpu.CompilerParams(vmem_limit_bytes=limit),
        cost_estimate=pl.CostEstimate(flops=flops, bytes_accessed=moved, transcendentals=0),
        name=name,
    )


def dot(a, b):
    return jnp.dot(a, b, preferred_element_type=F32)


def dot_t(a, b):
    return lax.dot_general(a, b, (((0,), (0,)), ((), ())), preferred_element_type=F32)


def fill(pick, tokens, wire):
    rows, band = tokens.shape
    t = tokens[...]
    wire[:, :band] = dot(pick[:, :rows], t).astype(BF)
    halves = jnp.concatenate([t[:, : band // 2], t[:, band // 2 :]], axis=0)
    wire[:, band:] = dot(pick[:, rows:], halves).astype(BF)


def lists_kernel(ids, probs, pick, mix):
    fanout, rows = ids.shape
    experts = pick.shape[0] // NEAR
    at = lax.broadcasted_iota(jnp.int32, (experts, rows), 0)
    place = {}
    for axis in TRADE[::-1]:
        place[axis] = at % EXPERT[axis]
        at = at // EXPERT[axis]
    label = jnp.zeros((experts, rows), jnp.int32)
    for axis, size in EXPERT.items():
        label = label * size + place[axis]
    p = probs[...]
    shares = (p / jnp.sum(p, axis=0, keepdims=True)).astype(BF).astype(F32)
    named = jnp.zeros((experts, rows), F32)
    share = jnp.zeros((experts, rows), F32)
    for k in range(fanout):
        hit = ids[k : k + 1, :] == label
        named = jnp.where(hit, 1.0, named)
        share = jnp.where(hit, shares[k : k + 1, :], share)
    i0 = lax.broadcasted_iota(jnp.int32, (rows, rows), 0)
    i1 = lax.broadcasted_iota(jnp.int32, (rows, rows), 1)
    before = dot(named.astype(BF), (i0 < i1).astype(F32).astype(BF))
    seat = jnp.where(named > 0.5, before, -1.0).astype(jnp.int32)

    def spread(values):
        return jnp.broadcast_to(values[:, None, :], (experts, NEAR, rows)).reshape(-1, rows)

    place = lax.broadcasted_iota(jnp.int32, (experts * NEAR, rows), 0) % NEAR
    seats = spread(seat)
    weights = spread(share)
    far = seats == place % FAR + NEAR
    for i, hit in enumerate((seats == place, far & (place < FAR), far & (place >= FAR))):
        pick[:, i * rows : (i + 1) * rows] = hit.astype(F32).astype(BF)
        if mix is not None:
            mix[:, i * rows : (i + 1) * rows] = jnp.where(hit, weights, 0.0).astype(BF)


def pick_kernel(ids, probs, tokens, wire, pick):
    lists_kernel(ids, probs, pick, None)
    fill(pick, tokens, wire)


def order(count):
    half = count // 2
    i = lax.broadcasted_iota(jnp.int32, (count, count), 0)
    j = lax.broadcasted_iota(jnp.int32, (count, count), 1)
    r = i % half
    return (j == (r // FAR) * (2 * FAR) + (i // half) * FAR + r % FAR).astype(F32).astype(BF)


def spread_far(far, wide):
    half = far.shape[0] // 2
    parts = []
    for i in range(far.shape[1] // wide):
        cols = slice(i * wide, (i + 1) * wide)
        parts += [far[:half, cols], far[half:, cols]]
    return jnp.concatenate(parts, axis=1)


def unpack(wires):
    count, width = wires[0].shape
    band = width // 3 * 2
    near = jnp.concatenate([w[:, :band] for w in wires], axis=1)
    far = jnp.concatenate([w[:, band:] for w in wires], axis=1)
    far = dot(order(count), far).astype(BF)
    return near, spread_far(far, band // 2)


def pack(near, far, down, wires):
    count, width = wires[0].shape
    band = width // 3 * 2
    wide = band // 2
    top, low = [], []
    for i, wire in enumerate(wires):
        cols = slice(i * band, (i + 1) * band)
        wire[:, :band] = dot(near, down[:, cols]).astype(BF)
        part = dot(far, down[:, cols]).astype(BF)
        top.append(part[:, :wide])
        low.append(part[:, wide:])
    both = jnp.concatenate([jnp.concatenate(top, axis=1), jnp.concatenate(low, axis=1)], axis=0)
    both = dot_t(order(count), both).astype(BF)
    for i, wire in enumerate(wires):
        wire[:, band:] = both[:, i * wide : (i + 1) * wide]


def band_at(k, parity, band):
    return pl.ds(pl.multiple_of((2 * (k % LINE) + parity) * band, band), band)


class Fetch:
    def __init__(self, sems):
        self.sems, self.copies = sems, []

    def __call__(self, src, dst):
        self.copies.append(pltpu.make_async_copy(src, dst, self.sems.at[len(self.copies)]))
        self.copies[-1].start()

    def up(self, wg, wu, dst, slot, rows):
        wide, band = wg.shape[1], rows.size
        to = pl.ds(slot * band, band)
        self(wg.at[rows, :], dst.at[to, pl.ds(0, wide)])
        self(wu.at[rows, :], dst.at[to, pl.ds(wide, wide)])

    def wait(self, first=0, last=None):
        for c in self.copies[first:last]:
            c.wait()


def place():
    return lax.axis_index("yh"), lax.axis_index("core")


def plus_kernel(wg, wu, *refs):
    wires, (out_near, out_far, up, x, y, near_sum, far_sum, sems) = refs[:6], refs[6:]
    yh, core = place()
    count, width = wires[0].shape
    band = up.shape[0] // 6
    wide = band // 2
    fetch = Fetch(sems)
    for i, wire in enumerate(wires):
        fetch(wire.at[:, pl.ds(band, wide)], y.at[:, pl.ds(i * wide, wide)])
    for i, wire in enumerate(wires):
        fetch(wire.at[:, pl.ds(0, band)], x.at[:, pl.ds(i * band, band)])
    for slot, (k, parity) in enumerate((k, p) for k in (0, 1, 3) for p in (core, 1 - core)):
        fetch.up(wg, wu, up, slot, band_at(yh + LINE - k, parity, band))
    seq = order(count)
    fetch.wait(0, 6)
    far = spread_far(dot(seq, y[...]).astype(BF), wide)
    fetch.wait(6)
    near_sum[...] = dot(x[...], up[...])
    back = Fetch(sems)
    back(near_sum, out_near)
    far_sum[...] = dot(far, up[...])
    back(far_sum, out_far)
    back.wait()


def load_kernel(wg, wu, wd, acc_near, acc_far, out_top, out_low, out_far, up, give13, give20, keep13, keep20, sems):
    yh, core = place()
    band = up.shape[0] // 2
    fetch = Fetch(sems)
    half = out_top.shape[0]
    fetch(acc_near.at[pl.ds(0, half), :], out_top)
    fetch(acc_near.at[pl.ds(half, half), :], out_low)
    fetch(acc_far, out_far)
    fetch.up(wg, wu, up, 0, band_at(yh + 2, core, band))
    fetch.up(wg, wu, up, 1, band_at(yh + 2, 1 - core, band))
    downs = ((give13, (1, 3), 1 - core), (give20, (2, 0), 1 - core), (keep13, (1, 3), core), (keep20, (2, 0), core))
    for down, ks, parity in downs:
        for slot, k in enumerate(ks):
            fetch(wd.at[:, band_at(yh + k, parity, band)], down.at[:, pl.ds(slot * band, band)])
    fetch.wait()


def halves(ref):
    rows = ref.shape[0] // 2
    return [ref.at[pl.ds(i * rows, rows), :] for i in range(2)]


def hidden_kernel(own, sib, acc_top, acc_low, acc_far, up, down, h, give):
    near, far = unpack((own, sib))
    n = near.shape[0]
    wide = h.shape[1]
    half = n // 2
    parts = (
        (near[:half], acc_top, slice(0, half)),
        (near[half:], acc_low, slice(half, n)),
        (far, acc_far, slice(n, h.shape[0])),
    )
    for x, acc, at in parts:
        both = acc[...] + dot(x, up[...])
        g, u = both[:, :wide], both[:, wide:]
        h[at, :] = (g / (1.0 + jnp.exp(-g)) * u).astype(BF)
    pack(h[:n, :], h[n:, :], down, halves(give))


def rest_kernel(h, give20, keep13, keep20, give, keep1, keep3, keep2, keep0):
    n = h.shape[0] // SEATS * NEAR
    near, far = h[:n, :], h[n:, :]
    pack(near, far, keep13, (keep1, keep3))
    pack(near, far, give20, halves(give))
    pack(near, far, keep20, (keep2, keep0))


def pair_kernel(keep1, keep3, give, one, three):
    for a, b, out in zip((keep1, keep3), halves(give), (one, three)):
        out[...] = (a[...].astype(F32) + b[...].astype(F32)).astype(BF)


def sum_kernel(keep0, give, one, three, out):
    total = keep0[...].astype(F32) + halves(give)[1][...].astype(F32)
    out[...] = (total + one[...].astype(F32) + three[...].astype(F32)).astype(BF)


def two_sum_kernel(keep2, give, out):
    out[...] = (keep2[...].astype(F32) + halves(give)[0][...].astype(F32)).astype(BF)


def mixed(mix, home):
    rows = mix.shape[1] // 3
    band = home.shape[1] // 3 * 2
    total = dot_t(mix[:, :rows], home[:, :band])
    rest = dot_t(mix[:, rows:], home[:, band:])
    return total + jnp.concatenate([rest[:rows], rest[rows:]], axis=1)


def mix_kernel(mix, home, out):
    out[...] = mixed(mix, home).astype(BF)


def last_kernel(mix, home, other, out):
    out[...] = (mixed(mix, home) + other[...].astype(F32)).astype(BF)


def body(tokens, expert_ids, router_probs, w_gate, w_up, w_down):
    rows, band = tokens.shape
    experts = lax.axis_size(TRADE)
    wide = w_gate.shape[2]
    lines = experts * NEAR

    def swap(x):
        return lax.ppermute(x, "core", [(0, 1), (1, 0)])

    def shift(x, k):
        return lax.ppermute(x, "yh", [(i, (i + k) % LINE) for i in range(LINE)])

    def trade(x):
        y = x.reshape(experts, NEAR, x.shape[1])
        y = lax.all_to_all(y, TRADE, split_axis=0, concat_axis=0, tiled=True)
        return y.reshape(x.shape)

    tie = lax.optimization_barrier
    wg, wu, wd = w_gate[0], w_up[0], w_down[0]
    width = band // 2 * 3
    wire, two = ((lines, width), BF), ((2 * lines, width), BF)
    sums = [((experts * n, 2 * wide), F32) for n in (NEAR, FAR)]
    lists = ((lines, 3 * rows), BF)
    work = 2 * experts * SEATS * band * wide
    sems = lambda n: pltpu.SemaphoreType.DMA((n,))
    other = shift(tokens, 2)
    (wire0,) = call(pick_kernel, [wire], "pick", [VM] * 3, limit=PICK_LIMIT, scratch=[pltpu.VMEM(*lists)])(
        expert_ids.T, router_probs.T, tokens
    )
    ids, wire0 = tie((expert_ids.T, wire0))
    pick, mix = call(lists_kernel, [lists] * 2, "lists", [VM] * 2, limit=PICK_LIMIT)(ids, router_probs.T)
    got0 = trade(wire0)
    (wire2,) = call(fill, [wire], "wire", [VM] * 2)(pick, other)
    got0, wire2 = tie((got0, wire2))
    got1, got3 = shift(got0, 1), shift(got0, 3)
    got2 = trade(wire2)
    sib0, sib1, sib3 = swap(got0), swap(got1), swap(got3)
    sums0 = call(
        plus_kernel,
        sums,
        "plus",
        [ANY] * 8,
        limit=PLUS_LIMIT,
        flops=SHORT,
        scratch=[
            pltpu.VMEM((6 * band, 2 * wide), BF),
            pltpu.VMEM((lines, 6 * band), BF),
            pltpu.VMEM((lines, 3 * band), BF),
        ]
        + [pltpu.VMEM(*x) for x in sums]
        + [sems(24)],
        out_specs=[HBM] * 2,
    )(wg, wu, got0, sib0, got1, sib1, got3, sib3)
    got2, sums0 = tie((got2, sums0))
    sib2 = swap(got2)
    pair = ((wide, 2 * band), BF)
    top, low, far, up2, give13, give20, keep13, keep20 = call(
        load_kernel,
        [((experts * FAR, 2 * wide), F32)] * 3 + [((2 * band, 2 * wide), BF)] + [pair] * 4,
        "load",
        [ANY, ANY, ANY, HBM, HBM],
        limit=LOAD_LIMIT,
        scratch=[sems(15)],
    )(wg, wu, wd, *sums0)
    h, give_a = call(
        hidden_kernel, [((experts * SEATS, wide), BF), two], "hidden", [VM] * 7, flops=6 * work
    )(got2, sib2, top, low, far, up2, give13)
    give_a = swap(give_a)
    give_b, keep1, keep3, keep2, keep0 = call(
        rest_kernel,
        [two] + [wire] * 4,
        "rest",
        [VM] * 4,
        limit=REST_LIMIT,
        flops=6 * work,
    )(h, give20, keep13, keep20)
    one, three = call(pair_kernel, [wire] * 2, "pair", [VM] * 3)(keep1, keep3, give_a)
    one, three, give_b = tie((one, three, give_b))
    one, three = shift(one, 1), shift(three, 3)
    give_b = swap(give_b)
    (back2,) = call(two_sum_kernel, [wire], "two_sum", [VM] * 2)(keep2, give_b)
    home2 = trade(back2)
    (back0,) = call(sum_kernel, [wire], "sum", [VM] * 4, flops=LONG)(keep0, give_b, one, three)
    home0 = trade(back0)
    (part,) = call(mix_kernel, [((rows, band), BF)], "mix", [VM] * 2)(mix, home2)
    (out,) = call(last_kernel, [((rows, band), BF)], "last", [VM] * 3)(mix, home0, shift(part, 2))
    return out


def solution(mesh):
    sizes = DP | EXPERT
    mesh = Mesh(mesh.devices.reshape(*sizes.values()), tuple(sizes))
    dp, expert = tuple(DP), tuple(EXPERT)
    return jax.shard_map(
        body,
        mesh=mesh,
        in_specs=(
            P(expert, dp),
            P(expert, None),
            P(expert, None),
            P(expert, None, dp),
            P(expert, None, dp),
            P(expert, dp, None),
        ),
        out_specs=P(expert, dp),
        check_vma=False,
    )
```
